32 devices in a mesh: lon: 8 (over y, x, core), lat: 4 (over z).
Axes of the slice: x: 2, y: 2, z: 4, core: 2. Of those that a mesh axis runs over, the one named last changes fastest.
Arguments:
- control: float32 [2, 16, 256, 1024], P(None, None, 'lat', 'lon'), may hold values from -6 to 6
- land_mask: int32 [256, 1024], P('lat', 'lon'), may hold values 0 or 1
- std_dev: float32 [2, 16], replicated, may hold values from 0.3 to 3
- innovation: float32 [32, 16, 1024], P(None, 'lat', 'lon'), may hold values from -6 to 6
- inverse_var: float32 [32, 16, 1024], P(None, 'lat', 'lon'), may hold values from 0.25 to 4
- obs_row: int32 [16, 1024], P('lat', 'lon'), may hold values from 0 to 62
- obs_col: int32 [16, 1024], P('lat', 'lon'), may hold values from 0 to 126
- frac_row: float32 [16, 1024], P('lat', 'lon'), may hold values from 0 to 1
- frac_col: float32 [16, 1024], P('lat', 'lon'), may hold values from 0 to 1
- counts: int32 [16, 64], P('lat', 'lon'), may hold values from 0 to 16, as said below
Outputs:
- gradient: float32 [2, 16, 256, 1024], P(None, None, 'lat', 'lon')
The draws below stay inside these ranges and needn't reach their ends.
Inputs may be any that keep to these rules, and one draw needn't show every extreme that they name: `counts`: each tile gets at most 16 live slots from one holder; in every draw some tile gets exactly 16 from every holder. Dense tiles are drawn from the seed.
All inputs are finite; a program needn't handle non-finite values. No bound on the sum of `land_mask` on one device may be relied on, other than what follows from the above.
Results may differ from the reference program's by a relative error of at most 0.000075.
Values sent between devices are 32-bit elements; how exact they have to be, the bound alone decides.
A program may use at most 64 MiB of HBM per device.

```python
import math
import jax
import jax.numpy as jnp
from jax import lax

LEV = 16
CY = 64
CX = 128
HALF = 50
CAP = 16
NY = 256
NX = 1024
N_LON = 8
N_LAT = 4


def draw_counts(key, part):
    density = jax.random.randint(jax.random.fold_in(key, 11), (N_LAT, 1, N_LON, 1), 1, 5)
    baseline = jax.random.randint(jax.random.fold_in(key, 12), (N_LAT, N_LAT, N_LON, N_LON), CAP // 4, CAP + 1)
    filled = jnp.minimum(baseline * density // 4, CAP)
    full_lat = jax.random.randint(jax.random.fold_in(key, 13), (), 0, N_LAT)
    full_lon = jax.random.randint(jax.random.fold_in(key, 14), (), 0, N_LON)
    lat_index = jnp.arange(N_LAT).reshape(N_LAT, 1, 1, 1)
    lon_index = jnp.arange(N_LON).reshape(1, 1, N_LON, 1)
    chosen = (lat_index == full_lat) & (lon_index == full_lon)
    filled = jnp.where(chosen, CAP, filled)
    return filled.reshape(N_LAT * N_LAT, N_LON * N_LON).astype(jnp.int32)


def place_ends(values, own_key, low, top_value):
    longest = values.shape.index(max(values.shape))
    spots = []
    for shift in (0, 1):
        where = [jax.random.randint(jax.random.fold_in(own_key, axis), (), 0, length) for axis, length in enumerate(values.shape)]
        where[longest] = (where[longest] + shift) % values.shape[longest]
        spots.append(tuple(where))
    return values.at[spots[0]].set(low).at[spots[1]].set(top_value)


def block_scale(rng, extent, shards, smallest, high):
    level = 1.0
    for dim, parts in shards:
        steps = jax.random.uniform(jax.random.fold_in(jax.random.fold_in(rng, 6), dim), (parts,), jnp.float32, smallest / len(shards), high / len(shards))
        level = level * jnp.repeat(jnp.exp(steps), extent[dim] // parts).reshape((-1,) + (1,) * (len(extent) - 1 - dim))
    return level


def gaussian(key, dims, scale, reach, pieces=(), held_as=jnp.bfloat16):
    gain = block_scale(key, dims, pieces, -0.22, 0.18) if pieces else 1.0
    entries = jax.random.normal(key, dims, jnp.float32) * scale * gain
    return jnp.minimum(jnp.maximum(entries, -reach), reach).astype(held_as)


def setup_inputs(seed: int = 0) -> dict:
    streams_of = jax.random.split(jax.random.key(seed), 11)
    return {
        "control": gaussian(streams_of[0], (2, LEV, NY, NX), 1.0, 6.0, ((2, 4), (3, 8)), jnp.float32),
        "land_mask": place_ends((jax.random.randint(streams_of[1], (NY, NX), 0, 10) < 7).astype(jnp.int32), jax.random.fold_in(streams_of[1], 1), 0, 1),
        "std_dev": jnp.clip(jnp.exp(jax.random.uniform(streams_of[2], (2, LEV), jnp.float32, math.log(0.3), math.log(3.0))), 0.3, 3.0),
        "innovation": gaussian(streams_of[3], (2 * LEV, N_LAT * N_LAT, N_LON * N_LON * CAP), 1.0, 6.0, ((1, 4), (2, 8)), jnp.float32),
        "inverse_var": jnp.clip(jnp.exp(math.log(4.0) - 2.7725887 * jax.random.uniform(streams_of[4], (2 * LEV, N_LAT * N_LAT, N_LON * N_LON * CAP), jnp.float32) ** block_scale(streams_of[4], (2 * LEV, N_LAT * N_LAT, N_LON * N_LON * CAP), ((1, 4), (2, 8)), -0.2, 0.2)), 0.25, 4.0),
        "obs_row": place_ends(jax.random.randint(streams_of[5], (N_LAT * N_LAT, N_LON * N_LON * CAP), 0, CY - 1), jax.random.fold_in(streams_of[5], 1), 0, (CY - 1) - 1).astype(jnp.int32),
        "obs_col": place_ends(jax.random.randint(streams_of[6], (N_LAT * N_LAT, N_LON * N_LON * CAP), 0, CX - 1), jax.random.fold_in(streams_of[6], 1), 0, (CX - 1) - 1).astype(jnp.int32),
        "frac_row": jnp.clip(1.0 * jax.random.uniform(streams_of[7], (N_LAT * N_LAT, N_LON * N_LON * CAP), jnp.float32) ** block_scale(streams_of[7], (N_LAT * N_LAT, N_LON * N_LON * CAP), ((0, 4), (1, 8)), -0.2, 0.2), 0.0, 1.0),
        "frac_col": jnp.clip(1.0 * jax.random.uniform(streams_of[8], (N_LAT * N_LAT, N_LON * N_LON * CAP), jnp.float32) ** block_scale(streams_of[8], (N_LAT * N_LAT, N_LON * N_LON * CAP), ((0, 4), (1, 8)), -0.2, 0.2), 0.0, 1.0),
        "counts": draw_counts(jax.random.fold_in(streams_of[10], 71), 0),
    }


def filter_taps(half_width):
    offsets = jnp.arange(-half_width, half_width + 1).astype(jnp.float32)
    spread = half_width / 2.0
    profile = jnp.exp(-0.5 * (offsets / spread) * (offsets / spread))
    return profile / jnp.sqrt(jnp.sum(profile * profile))

def run_filter(extended, along_rows):
    taps_vector = filter_taps(HALF)
    if along_rows:
        kernel = taps_vector.reshape(1, 1, -1, 1)
    else:
        kernel = taps_vector.reshape(1, 1, 1, -1)
    output = lax.conv_general_dilated(extended[:, None], kernel, (1, 1), 'VALID', dimension_numbers=('NCHW', 'OIHW', 'NCHW'), precision=lax.Precision.HIGHEST)
    return output[:, 0]

def along_x(field):
    extended = jnp.concatenate([field[:, :, -HALF:], field, field[:, :, :HALF]], axis=2)
    return run_filter(extended, False)

def along_y(field):
    extended = jnp.pad(field, ((0, 0), (HALF, HALF), (0, 0)))
    return run_filter(extended, True)

def to_owner_order(values, rows_total):
    shaped = values.reshape(rows_total, N_LAT, N_LAT, N_LON, N_LON, CAP)
    return shaped.transpose(0, 2, 1, 4, 3, 5).reshape(rows_total, -1)

def reference(control, land_mask, std_dev, innovation, inverse_var, obs_row, obs_col, frac_row, frac_col, counts):
    rows_total = 2 * LEV
    fields = control.reshape(rows_total, NY, NX)
    ocean = land_mask.astype(jnp.float32)
    scales = std_dev.reshape(rows_total, 1, 1)
    increment = scales * ocean * along_y(along_x(ocean * fields))
    table = increment.reshape(rows_total, NY * NX)
    lat_start = (jnp.arange(N_LAT) * CY).astype(jnp.int32).reshape(N_LAT, 1, 1, 1, 1)
    lon_start = (jnp.arange(N_LON) * CX).astype(jnp.int32).reshape(1, 1, N_LON, 1, 1)
    grid_row = obs_row.reshape(N_LAT, N_LAT, N_LON, N_LON, CAP) + lat_start
    grid_col = obs_col.reshape(N_LAT, N_LAT, N_LON, N_LON, CAP) + lon_start
    corner = (grid_row * NX + grid_col).reshape(-1).astype(jnp.int32)
    row_part = frac_row.reshape(-1)
    col_part = frac_col.reshape(-1)
    stencil = [(1.0 - row_part) * (1.0 - col_part), (1.0 - row_part) * col_part, row_part * (1.0 - col_part), row_part * col_part]
    shifts = [0, 1, NX, NX + 1]
    columns = jnp.zeros((rows_total, corner.shape[0]), jnp.float32)
    for weight, offset in zip(stencil, shifts):
        columns = columns + weight[None, :] * jnp.take(table, corner + offset, axis=1)
    live_slots = counts.reshape(N_LAT, N_LAT, N_LON, N_LON, 1) > jnp.arange(CAP).astype(jnp.int32).reshape(1, 1, 1, 1, CAP)
    live = live_slots.reshape(-1).astype(jnp.float32)
    misfit = to_owner_order(inverse_var, rows_total) * (columns - to_owner_order(innovation, rows_total)) * live[None, :]
    index_all = jnp.concatenate([corner + offset for offset in shifts])
    values_all = jnp.concatenate([weight[None, :] * misfit for weight in stencil], axis=1)
    spread = jnp.zeros((rows_total, NY * NX), jnp.float32).at[:, index_all].add(values_all)
    weighted = spread.reshape(rows_total, NY, NX) * scales
    gradient = fields + ocean * along_x(along_y(ocean * weighted))
    return gradient.reshape(2, LEV, NY, NX)
```

```python
import jax
import jax.numpy as jnp
from jax import lax
from jax.sharding import PartitionSpec as P

HALF = 50


def padded_2(cells, sides, width):
    for axis, dim in sides:
        count = lax.axis_size(axis)
        head = lax.slice_in_dim(cells, 0, width, axis=dim)
        tail = lax.slice_in_dim(cells, cells.shape[dim] - width, cells.shape[dim], axis=dim)
        cells = jnp.concatenate(
            [
                lax.ppermute(tail, axis, [(i, (i + 1) % count) for i in range(count)]),
                cells,
                lax.ppermute(head, axis, [((i + 1) % count, i) for i in range(count)]),
            ],
            axis=dim,
        )
    return cells


def tap_band(n_out, n_in, offset):
    spread = HALF / 2.0
    whole = jnp.arange(-HALF, HALF + 1).astype(jnp.float32)
    norm = jnp.sqrt(jnp.sum(jnp.exp(-(whole / spread) * (whole / spread))))
    out_index = lax.broadcasted_iota(jnp.int32, (n_out, n_in), 0)
    in_index = lax.broadcasted_iota(jnp.int32, (n_out, n_in), 1)
    reach = in_index - out_index - offset
    inside = (reach >= 0) & (reach <= 2 * HALF)
    distance = (reach - HALF).astype(jnp.float32)
    values = jnp.exp(-0.5 * (distance / spread) * (distance / spread)) / norm
    return jnp.where(inside, values, 0.0)


def along_x(field):
    extended = padded_2(field, (("lon", 2),), HALF)
    width = field.shape[2]
    band = tap_band(width, width + 2 * HALF, 0)
    return jnp.einsum("rye,xe->ryx", extended, band, precision=lax.Precision.HIGHEST)


def along_y(field):
    count = lax.axis_size("lat")
    height = field.shape[1]
    below = lax.ppermute(field[:, height - HALF :], "lat", [(i, i + 1) for i in range(count - 1)])
    above = lax.ppermute(field[:, :HALF], "lat", [(i + 1, i) for i in range(count - 1)])
    extended = jnp.concatenate([below, field, above], axis=1)
    band = tap_band(height, height + 2 * HALF, 0)
    return jnp.einsum("ye,rex->ryx", band, extended, precision=lax.Precision.HIGHEST)


def to_owner(values):
    return lax.all_to_all(
        lax.all_to_all(values, "lon", split_axis=2, concat_axis=2, tiled=True),
        "lat",
        split_axis=1,
        concat_axis=1,
        tiled=True,
    )


def shards(
    control,
    land_mask,
    std_dev,
    innovation,
    inverse_var,
    obs_row,
    obs_col,
    frac_row,
    frac_col,
    counts,
):
    rows_total = control.shape[0] * control.shape[1]
    tile_rows = control.shape[2]
    tile_cols = control.shape[3]
    fields = control.reshape(rows_total, tile_rows, tile_cols)
    ocean = land_mask.astype(jnp.float32)
    scales = std_dev.reshape(rows_total, 1, 1)
    increment = scales * ocean * along_y(along_x(ocean * fields))
    table = increment.reshape(rows_total, tile_rows * tile_cols)
    corner = obs_row * tile_cols + obs_col
    stencil = [
        (1.0 - frac_row) * (1.0 - frac_col),
        (1.0 - frac_row) * frac_col,
        frac_row * (1.0 - frac_col),
        frac_row * frac_col,
    ]
    shifts = [0, 1, tile_cols, tile_cols + 1]
    columns = jnp.zeros((rows_total,) + corner.shape, jnp.float32)
    for weight, offset in zip(stencil, shifts):
        columns = columns + weight[None] * jnp.take(table, corner + offset, axis=1)
    owned = to_owner(jnp.concatenate([innovation, inverse_var], axis=0))
    at_owner = owned[rows_total:] * (columns - owned[:rows_total])
    slot_width = obs_row.shape[1] // counts.shape[1]
    slot_number = lax.broadcasted_iota(jnp.int32, obs_row.shape, 1) % slot_width
    limits = jnp.repeat(counts, slot_width, axis=1)
    live = (slot_number < limits).astype(jnp.float32)
    misfit = at_owner * live[None]
    index_all = jnp.concatenate([(corner + offset).reshape(-1) for offset in shifts])
    values_all = jnp.concatenate(
        [(weight[None] * misfit).reshape(rows_total, -1) for weight in stencil], axis=1
    )
    spread = (
        jnp.zeros((rows_total, tile_rows * tile_cols), jnp.float32).at[:, index_all].add(values_all)
    )
    weighted = spread.reshape(rows_total, tile_rows, tile_cols) * scales
    gradient = fields + ocean * along_x(along_y(ocean * weighted))
    return gradient.reshape(control.shape)


def solution(mesh):
    in_specs = (
        P(None, None, "lat", "lon"),
        P("lat", "lon"),
        P(),
        P(None, "lat", "lon"),
        P(None, "lat", "lon"),
        P("lat", "lon"),
        P("lat", "lon"),
        P("lat", "lon"),
        P("lat", "lon"),
        P("lat", "lon"),
    )
    out_specs = P(None, None, "lat", "lon")
    return jax.shard_map(shards, mesh=mesh, in_specs=in_specs, out_specs=out_specs, check_vma=False)
```

```python
import functools

import jax
import jax.numpy as jnp
import numpy as np
from jax import lax
from jax.experimental import pallas as pl
from jax.experimental.pallas import tpu as pltpu
from jax.sharding import PartitionSpec as P

HALF = 50
SPREAD = HALF / 2.0
_TAPS = np.exp(-0.5 * (np.arange(-HALF, HALF + 1) / SPREAD) ** 2)
NORM = float(1.0 / np.sqrt(np.sum(_TAPS * _TAPS)))
CHUNK = 512
GROUP = 8
VMEM_LIMIT = 48 * 1024 * 1024
VMEM = pl.BlockSpec(memory_space=pltpu.VMEM)


def split(x):
    hi = x.astype(jnp.bfloat16)
    lo = (x - hi.astype(jnp.float32)).astype(jnp.bfloat16)
    return hi, lo


def taps(distance):
    values = jnp.exp(distance * distance * (-0.5 / (SPREAD * SPREAD))) * NORM
    return jnp.where(jnp.abs(distance) < HALF + 0.5, values, 0.0)


def iota(shape, dim):
    return lax.broadcasted_iota(jnp.int32, shape, dim).astype(jnp.float32)


def meta_kernel(mask_ref, row_ref, col_ref, frow_ref, fcol_ref, counts_ref, out_ref):
    mask = mask_ref[...].astype(jnp.bfloat16)
    height, width = mask.shape
    holders, lanes = row_ref.shape
    tiles = counts_ref.shape[1]
    cap = lanes // tiles
    tile = lax.broadcasted_iota(jnp.int32, (tiles, lanes), 0)
    lane = lax.broadcasted_iota(jnp.int32, (tiles, lanes), 1)
    inside = (lane >= tile * cap) & (lane < tile * cap + cap)
    repeat = jnp.where(inside, 1.0, 0.0).astype(jnp.bfloat16)
    first = jnp.sum(jnp.where(inside, tile * cap, 0).astype(jnp.float32), axis=0, keepdims=True)
    number = iota((1, lanes), 1) - first
    limits = jnp.dot(
        counts_ref[...].astype(jnp.float32).astype(jnp.bfloat16),
        repeat,
        preferred_element_type=jnp.float32,
    )
    for s in range(holders):
        row = row_ref[pl.ds(s, 1), :].astype(jnp.float32)
        col = col_ref[pl.ds(s, 1), :].astype(jnp.float32)
        a = frow_ref[pl.ds(s, 1), :]
        b = fcol_ref[pl.ds(s, 1), :]
        x = iota((width, lanes), 0) - col
        at_left = jnp.where(x == 0.0, 1.0, 0.0).astype(jnp.bfloat16)
        at_right = jnp.where(x == 1.0, 1.0, 0.0).astype(jnp.bfloat16)
        left = jnp.dot(mask, at_left, preferred_element_type=jnp.float32)
        right = jnp.dot(mask, at_right, preferred_element_type=jnp.float32)
        y = iota((height, lanes), 0) - row
        m00 = jnp.sum(jnp.where(y == 0.0, left, 0.0), axis=0, keepdims=True)
        m01 = jnp.sum(jnp.where(y == 0.0, right, 0.0), axis=0, keepdims=True)
        m10 = jnp.sum(jnp.where(y == 1.0, left, 0.0), axis=0, keepdims=True)
        m11 = jnp.sum(jnp.where(y == 1.0, right, 0.0), axis=0, keepdims=True)
        live = jnp.where(number < limits[s : s + 1], 1.0, 0.0)
        at = pl.ds(s * lanes, lanes)
        out_ref[0:1, at] = row
        out_ref[1:2, at] = col
        out_ref[2:3, at] = (1.0 - a) * (1.0 - b) * m00
        out_ref[3:4, at] = (1.0 - a) * b * m01
        out_ref[4:5, at] = a * (1.0 - b) * m10
        out_ref[5:6, at] = a * b * m11
        out_ref[6:7, at] = live
        out_ref[7:8, at] = live


def neighbours(n_lon, n_lat):
    lon, lat = lax.axis_index("lon"), lax.axis_index("lat")
    found = []
    for t in range(9):
        if t == 4:
            continue
        dp, dq = t // 3 - 1, t % 3 - 1
        there = (lat + dp >= 0) & (lat + dp < n_lat)
        target = {"lon": lax.rem(lon + dq + n_lon, n_lon), "lat": lat + dp}
        found.append((t, there, target, dp))
    return found


def guarded(dp, there, body):
    if dp == 0:
        body()
    else:
        pl.when(there)(body)


def greet(near):
    barrier = pltpu.get_barrier_semaphore()
    for _, there, target, dp in near:
        guarded(dp, there, lambda target=target: pl.semaphore_signal(barrier, inc=1, device_id=target))
    peers = sum(jnp.where(there, 1, 0) for _, there, _, _ in near)
    pl.semaphore_wait(barrier, peers)


def exchange(near, source, target_ref, send_sem, recv_sem):
    copies = []
    for t, there, target, dp in near:
        copy = pltpu.make_async_remote_copy(
            src_ref=source(t),
            dst_ref=target_ref.at[8 - t],
            send_sem=send_sem.at[t],
            recv_sem=recv_sem.at[8 - t],
            device_id=target,
        )
        guarded(dp, there, copy.start)
        copies.append((t, there, dp, copy))
    return copies


def finish(near, copies, target_ref, recv_sem):
    for t, there, dp, copy in copies:
        guarded(dp, there, copy.wait_send)
    for t, there, target, dp in near:
        arrival = pltpu.make_async_remote_copy(
            src_ref=target_ref.at[t],
            dst_ref=target_ref.at[t],
            send_sem=recv_sem.at[t],
            recv_sem=recv_sem.at[t],
            device_id=target,
        )
        guarded(dp, there, arrival.wait_recv)


def clear_missing(near, ref):
    for t, there, _, dp in near:
        if dp == 0:
            continue

        @pl.when(jnp.logical_not(there))
        def _():
            ref[t] = jnp.zeros(ref.shape[1:], ref.dtype)


def share_kernel(n_lon, n_lat, meta_ref, out_ref, send_sem, recv_sem):
    near = neighbours(n_lon, n_lat)
    greet(near)
    copies = exchange(near, lambda t: meta_ref, out_ref, send_sem, recv_sem)
    out_ref[4] = meta_ref[...]
    clear_missing(near, out_ref)
    finish(near, copies, out_ref, recv_sem)


def misfit_kernel(
    n_lon, n_lat, part_ref, owned_ref, meta_ref, std_ref, out_ref,
    landed, mine, send_sem, recv_sem, send_sem_2, recv_sem_2,
):
    near = neighbours(n_lon, n_lat)
    greet(near)
    copies = exchange(near, lambda t: part_ref.at[t], landed, send_sem, recv_sem)
    clear_missing(near, landed)
    clear_missing(near, out_ref)
    finish(near, copies, landed, recv_sem)
    total = part_ref[4]
    for t in range(9):
        if t != 4:
            total = total + landed[t]
    rows = total.shape[0]
    scale = std_ref[...]
    live = meta_ref[6:7, :]
    mine[...] = scale * owned_ref[rows:, :] * (scale * total - owned_ref[:rows, :]) * live
    out_ref[4] = mine[...]
    copies = exchange(near, lambda t: mine, out_ref, send_sem_2, recv_sem_2)
    finish(near, copies, out_ref, recv_sem_2)


def tables(meta, t, height, width):
    dp = (t // 3 - 1).astype(jnp.float32) * height
    dq = (t % 3 - 1).astype(jnp.float32) * width
    chunk = meta.shape[1]
    y = meta[0:1] + dp - iota((height, chunk), 0)
    x = meta[1:2] + dq - iota((width, chunk), 0)
    along_y = [taps(y), taps(y + 1.0)]
    left, right = taps(x), taps(x + 1.0)
    along_x = [
        meta[2:3] * left + meta[3:4] * right,
        meta[4:5] * left + meta[5:6] * right,
    ]
    return along_y, along_x


def forward_kernel(meta_ref, control_ref, mask_ref, out_ref, lhs, ys, xs):
    t = pl.program_id(0)
    levels, height, width = control_ref.shape

    @pl.when((t == 0) & (pl.program_id(1) == 0))
    def _():
        mask = mask_ref[...].astype(jnp.float32)

        @pl.loop(0, levels)
        def _(l):
            hi, lo = split(control_ref[l] * mask)
            at = pl.ds(pl.multiple_of(l * height, height), height)
            lhs[at, 0:width] = hi
            lhs[at, width : 2 * width] = hi
            lhs[at, 2 * width : 3 * width] = lo

    along_y, along_x = tables(meta_ref[0], t, height, width)
    for i in range(2):
        ys[i] = along_y[i]
        hi, lo = split(along_x[i])
        xs[i, 0:width] = hi
        xs[i, width : 2 * width] = lo
        xs[i, 2 * width : 3 * width] = hi

    rows = GROUP * height

    @pl.loop(0, levels // GROUP)
    def _(g):
        left = lhs[pl.ds(pl.multiple_of(g * rows, rows), rows), :]
        total = None
        for i in range(2):
            wide = jnp.dot(left, xs[i], preferred_element_type=jnp.float32)
            term = jnp.sum(wide.reshape(GROUP, height, -1) * ys[i][None], axis=1)
            total = term if total is None else total + term
        out_ref[0, pl.ds(pl.multiple_of(g * GROUP, GROUP), GROUP), :] = total


def backward_kernel(meta_ref, v_ref, control_ref, mask_ref, out_ref, ys, xs):
    t, c = pl.program_id(0), pl.program_id(1)
    levels, height, width = control_ref.shape

    @pl.when((t == 0) & (c == 0))
    def _():
        out_ref[...] = jnp.zeros_like(out_ref)

    along_y, along_x = tables(meta_ref[0], t, height, width)
    chunk = along_x[0].shape[1]
    for i in range(2):
        ys[i] = along_y[i]
        hi, lo = split(along_x[i])
        xs[0:width, i * chunk : (i + 1) * chunk] = hi
        xs[width : 2 * width, i * chunk : (i + 1) * chunk] = lo

    contract = (((1,), (1,)), ((), ()))

    @pl.loop(0, levels // GROUP)
    def _(g):
        at = pl.ds(pl.multiple_of(g * GROUP, GROUP), GROUP)
        v = v_ref[0, at, :]
        his, los = [], []
        for i in range(2):
            b = (v[:, None, :] * ys[i][None]).reshape(GROUP * height, chunk)
            hi, lo = split(b)
            his.append(hi)
            los.append(lo)
        wide = lax.dot_general(
            jnp.concatenate(his, axis=1), xs[...], contract, preferred_element_type=jnp.float32
        )
        rest = lax.dot_general(
            jnp.concatenate(los, axis=1), xs[0:width, :], contract, preferred_element_type=jnp.float32
        )
        total = wide[:, :width] + wide[:, width:] + rest
        out_ref[at] += total.reshape(GROUP, height, width)

    @pl.when((t == pl.num_programs(0) - 1) & (c == pl.num_programs(1) - 1))
    def _():
        mask = mask_ref[...].astype(jnp.float32)

        @pl.loop(0, levels)
        def _(l):
            out_ref[l] = control_ref[l] + mask * out_ref[l]


def to_owner(values):
    return lax.all_to_all(
        lax.all_to_all(values, "lon", split_axis=2, concat_axis=2, tiled=True),
        "lat",
        split_axis=1,
        concat_axis=1,
        tiled=True,
    )


def shards(
    n_lon, n_lat, control, land_mask, std_dev, innovation, inverse_var,
    obs_row, obs_col, frac_row, frac_col, counts,
):
    levels = control.shape[0] * control.shape[1]
    height, width = control.shape[2:]
    slots = obs_row.shape[0] * obs_row.shape[1]
    chunk = min(CHUNK, slots)
    fields = control.reshape(levels, height, width)
    scales = std_dev.reshape(levels, 1)
    f32 = jnp.float32
    params = functools.partial(pltpu.CompilerParams, vmem_limit_bytes=VMEM_LIMIT)
    sems = pltpu.SemaphoreType.DMA((9,))

    meta = pl.pallas_call(
        meta_kernel,
        out_shape=jax.ShapeDtypeStruct((8, slots), f32),
        in_specs=[VMEM] * 6,
        out_specs=VMEM,
        compiler_params=params(),
        name="slot_weights",
    )(land_mask, obs_row, obs_col, frac_row, frac_col, counts)
    meta_all = pl.pallas_call(
        functools.partial(share_kernel, n_lon, n_lat),
        out_shape=jax.ShapeDtypeStruct((9, 8, slots), f32),
        in_specs=[VMEM],
        out_specs=VMEM,
        scratch_shapes=[sems, sems],
        compiler_params=params(collective_id=0, has_side_effects=True),
        name="share_slots",
    )(meta)

    owned = to_owner(jnp.concatenate([innovation, inverse_var], axis=0)).reshape(2 * levels, slots)

    grid = (9, slots // chunk)
    meta_spec = pl.BlockSpec((1, 8, chunk), lambda t, c: (t, 0, c))
    slot_spec = pl.BlockSpec((1, levels, chunk), lambda t, c: (t, 0, c))
    field_spec = pl.BlockSpec((levels, height, width), lambda t, c: (0, 0, 0))
    mask_spec = pl.BlockSpec((height, width), lambda t, c: (0, 0))
    parts = pl.pallas_call(
        forward_kernel,
        grid=grid,
        out_shape=jax.ShapeDtypeStruct((9, levels, slots), f32),
        in_specs=[meta_spec, field_spec, mask_spec],
        out_specs=slot_spec,
        scratch_shapes=[
            pltpu.VMEM((levels * height, 3 * width), jnp.bfloat16),
            pltpu.VMEM((2, height, chunk), f32),
            pltpu.VMEM((2, 3 * width, chunk), jnp.bfloat16),
        ],
        compiler_params=params(),
        name="partial_columns",
    )(meta_all, fields, land_mask)

    scaled = pl.pallas_call(
        functools.partial(misfit_kernel, n_lon, n_lat),
        out_shape=jax.ShapeDtypeStruct((9, levels, slots), f32),
        in_specs=[VMEM] * 4,
        out_specs=VMEM,
        scratch_shapes=[
            pltpu.VMEM((9, levels, slots), f32),
            pltpu.VMEM((levels, slots), f32),
            sems, sems, sems, sems,
        ],
        compiler_params=params(collective_id=1, has_side_effects=True),
        name="misfits",
    )(parts, owned, meta, scales)

    gradient = pl.pallas_call(
        backward_kernel,
        grid=grid,
        out_shape=jax.ShapeDtypeStruct((levels, height, width), f32),
        in_specs=[meta_spec, slot_spec, field_spec, mask_spec],
        out_specs=field_spec,
        scratch_shapes=[
            pltpu.VMEM((2, height, chunk), f32),
            pltpu.VMEM((2 * width, 2 * chunk), jnp.bfloat16),
        ],
        compiler_params=params(),
        name="gradient",
    )(meta_all, scaled, fields, land_mask)
    return gradient.reshape(control.shape)


def solution(mesh):
    tile = P("lat", "lon")
    in_specs = (
        P(None, None, "lat", "lon"), tile, P(),
        P(None, "lat", "lon"), P(None, "lat", "lon"),
        tile, tile, tile, tile, tile,
    )
    body = functools.partial(shards, mesh.shape["lon"], mesh.shape["lat"])
    return jax.shard_map(
        body, mesh=mesh, in_specs=in_specs,
        out_specs=P(None, None, "lat", "lon"), check_vma=False,
    )
```

```python
import functools

import jax
import jax.numpy as jnp
import numpy as np
from jax import lax
from jax.experimental import pallas as pl
from jax.experimental.pallas import tpu as pltpu
from jax.sharding import PartitionSpec as P

HALF = 50
SPREAD = HALF / 2.0
_TAPS = np.exp(-0.5 * (np.arange(-HALF, HALF + 1) / SPREAD) ** 2)
NORM = float(1.0 / np.sqrt(np.sum(_TAPS * _TAPS)))
CHUNK = 128
GROUP = 8
VMEM_LIMIT = 48 * 1024 * 1024
VMEM = pl.BlockSpec(memory_space=pltpu.VMEM)


def split(x):
    hi = x.astype(jnp.bfloat16)
    lo = (x - hi.astype(jnp.float32)).astype(jnp.bfloat16)
    return hi, lo


def taps(distance):
    values = jnp.exp(distance * distance * (-0.5 / (SPREAD * SPREAD))) * NORM
    return jnp.where(jnp.abs(distance) < HALF + 0.5, values, 0.0)


def iota(shape, dim):
    return lax.broadcasted_iota(jnp.int32, shape, dim).astype(jnp.float32)


def arrange(values, rank, out_ref):
    hi = values.astype(jnp.bfloat16)
    low, least = split(values - hi.astype(jnp.float32))
    parts = jnp.concatenate([hi.astype(jnp.float32), low.astype(jnp.float32), least.astype(jnp.float32)], axis=0)
    parts = parts.astype(jnp.bfloat16)
    count, slots = values.shape
    for k in range(slots // CHUNK):
        place = iota((CHUNK, slots), 0) + float(k * CHUNK)
        one = jnp.where(place == rank, 1.0, 0.0).astype(jnp.bfloat16)
        moved = lax.dot_general(
            parts, one, (((1,), (1,)), ((), ())), preferred_element_type=jnp.float32
        )
        out_ref[:, k * CHUNK : (k + 1) * CHUNK] = (
            moved[:count] + moved[count : 2 * count] + moved[2 * count :]
        )


def meta_kernel(mask_ref, row_ref, col_ref, frow_ref, fcol_ref, counts_ref, out_ref, rank_ref, raw):
    mask = mask_ref[...].astype(jnp.bfloat16)
    height, width = mask.shape
    holders, lanes = row_ref.shape
    tiles = counts_ref.shape[1]
    cap = lanes // tiles
    tile = lax.broadcasted_iota(jnp.int32, (tiles, lanes), 0)
    lane = lax.broadcasted_iota(jnp.int32, (tiles, lanes), 1)
    inside = (lane >= tile * cap) & (lane < tile * cap + cap)
    repeat = jnp.where(inside, 1.0, 0.0).astype(jnp.bfloat16)
    first = jnp.sum(jnp.where(inside, tile * cap, 0).astype(jnp.float32), axis=0, keepdims=True)
    number = iota((1, lanes), 1) - first
    limits = jnp.dot(
        counts_ref[...].astype(jnp.float32).astype(jnp.bfloat16),
        repeat,
        preferred_element_type=jnp.float32,
    )
    for s in range(holders):
        row = row_ref[pl.ds(s, 1), :].astype(jnp.float32)
        col = col_ref[pl.ds(s, 1), :].astype(jnp.float32)
        a = frow_ref[pl.ds(s, 1), :]
        b = fcol_ref[pl.ds(s, 1), :]
        x = iota((width, lanes), 0) - col
        at_left = jnp.where(x == 0.0, 1.0, 0.0).astype(jnp.bfloat16)
        at_right = jnp.where(x == 1.0, 1.0, 0.0).astype(jnp.bfloat16)
        left = jnp.dot(mask, at_left, preferred_element_type=jnp.float32)
        right = jnp.dot(mask, at_right, preferred_element_type=jnp.float32)
        y = iota((height, lanes), 0) - row
        m00 = jnp.sum(jnp.where(y == 0.0, left, 0.0), axis=0, keepdims=True)
        m01 = jnp.sum(jnp.where(y == 0.0, right, 0.0), axis=0, keepdims=True)
        m10 = jnp.sum(jnp.where(y == 1.0, left, 0.0), axis=0, keepdims=True)
        m11 = jnp.sum(jnp.where(y == 1.0, right, 0.0), axis=0, keepdims=True)
        live = jnp.where(number < limits[s : s + 1], 1.0, 0.0)
        at = pl.ds(s * lanes, lanes)
        raw[0:1, at] = row
        raw[1:2, at] = col
        raw[2:3, at] = (1.0 - a) * (1.0 - b) * m00 * live
        raw[3:4, at] = (1.0 - a) * b * m01 * live
        raw[4:5, at] = a * (1.0 - b) * m10 * live
        raw[5:6, at] = a * b * m11 * live
        raw[6:7, at] = live
        raw[7:8, at] = live


    slots = raw.shape[1]
    order = jnp.where(raw[6:7, :] > 0.0, raw[1:2, :], float(width)) * slots + iota((1, slots), 1)
    eye = iota((CHUNK, CHUNK), 0) == iota((CHUNK, CHUNK), 1)
    rank = jnp.zeros((1, slots), jnp.float32)
    for k in range(slots // CHUNK):
        piece = order[:, k * CHUNK : (k + 1) * CHUNK]
        column = jnp.sum(jnp.where(eye, piece, 0.0), axis=1, keepdims=True)
        rank = rank + jnp.sum(jnp.where(column < order, 1.0, 0.0), axis=0, keepdims=True)
    rank_ref[...] = rank
    arrange(raw[...], rank, out_ref)


def neighbours(n_lon, n_lat):
    lon, lat = lax.axis_index("lon"), lax.axis_index("lat")
    found = []
    for t in range(9):
        if t == 4:
            continue
        dp, dq = t // 3 - 1, t % 3 - 1
        there = (lat + dp >= 0) & (lat + dp < n_lat)
        target = {"lon": lax.rem(lon + dq + n_lon, n_lon), "lat": lat + dp}
        found.append((t, there, target, dp))
    return found


def guarded(dp, there, body):
    if dp == 0:
        body()
    else:
        pl.when(there)(body)


def greet(near):
    barrier = pltpu.get_barrier_semaphore()
    for _, there, target, dp in near:
        guarded(dp, there, lambda target=target: pl.semaphore_signal(barrier, inc=1, device_id=target))
    peers = sum(jnp.where(there, 1, 0) for _, there, _, _ in near)
    pl.semaphore_wait(barrier, peers)


def exchange(near, source, target_ref, send_sem, recv_sem):
    copies = []
    for t, there, target, dp in near:
        copy = pltpu.make_async_remote_copy(
            src_ref=source(t),
            dst_ref=target_ref.at[8 - t],
            send_sem=send_sem.at[t],
            recv_sem=recv_sem.at[8 - t],
            device_id=target,
        )
        guarded(dp, there, copy.start)
        copies.append((t, there, dp, copy))
    return copies


def finish(near, copies, target_ref, recv_sem):
    for t, there, dp, copy in copies:
        guarded(dp, there, copy.wait_send)
    for t, there, target, dp in near:
        arrival = pltpu.make_async_remote_copy(
            src_ref=target_ref.at[t],
            dst_ref=target_ref.at[t],
            send_sem=recv_sem.at[t],
            recv_sem=recv_sem.at[t],
            device_id=target,
        )
        guarded(dp, there, arrival.wait_recv)


def clear_missing(near, ref):
    for t, there, _, dp in near:
        if dp == 0:
            continue

        @pl.when(jnp.logical_not(there))
        def _():
            ref[t] = jnp.zeros(ref.shape[1:], ref.dtype)


def share_kernel(n_lon, n_lat, meta_ref, out_ref, send_sem, recv_sem):
    near = neighbours(n_lon, n_lat)
    greet(near)
    copies = exchange(near, lambda t: meta_ref, out_ref, send_sem, recv_sem)
    out_ref[4] = meta_ref[...]
    clear_missing(near, out_ref)
    finish(near, copies, out_ref, recv_sem)


def misfit_kernel(
    n_lon, n_lat, part_ref, owned_ref, meta_ref, rank_ref, std_ref, out_ref,
    landed, mine, placed, send_sem, recv_sem, send_sem_2, recv_sem_2,
):
    near = neighbours(n_lon, n_lat)
    greet(near)
    copies = exchange(near, lambda t: part_ref.at[t], landed, send_sem, recv_sem)
    clear_missing(near, landed)
    clear_missing(near, out_ref)
    arrange(owned_ref[...], rank_ref[...], placed)
    finish(near, copies, landed, recv_sem)
    total = part_ref[4]
    for t in range(9):
        if t != 4:
            total = total + landed[t]
    rows = total.shape[0]
    scale = std_ref[...]
    live = meta_ref[6:7, :]
    mine[...] = scale * placed[rows:, :] * (scale * total - placed[:rows, :]) * live
    out_ref[4] = mine[...]
    copies = exchange(near, lambda t: mine, out_ref, send_sem_2, recv_sem_2)
    finish(near, copies, out_ref, recv_sem_2)


def tables(meta, shift_y, shift_x, height, width, first):
    chunk = meta.shape[1]
    y = meta[0:1] + shift_y - iota((height, chunk), 0)
    x = meta[1:2] + shift_x - first - iota((width, chunk), 0)
    left, right = taps(x), taps(x + 1.0)
    along_x = [
        meta[2:3] * left + meta[3:4] * right,
        meta[4:5] * left + meta[5:6] * right,
    ]
    return [taps(y), taps(y + 1.0)], along_x


def walk(meta_ref, height, width, work, skip=None):
    chunks = meta_ref.shape[2] // CHUNK
    near_cols = width // 2 if HALF <= width // 2 else width
    for dq in (-1, 0, 1):
        cols = near_cols if dq else width
        first = width - cols if dq > 0 else 0

        @pl.loop(0, 3 * chunks)
        def _(step):
            p, c = lax.div(step, chunks), lax.rem(step, chunks)
            t = 3 * p + (dq + 1)
            at = pl.ds(pl.multiple_of(c * CHUNK, CHUNK), CHUNK)
            meta = meta_ref[t, :, at]
            shift_y = (p - 1).astype(jnp.float32) * height
            shift_x = float(dq * width)
            y, x = meta[0:1] + shift_y, meta[1:2] + shift_x
            reached = (
                (y >= -(HALF + 1.0)) & (y <= height - 1.0 + HALF)
                & (x >= -(HALF + 1.0)) & (x <= width - 1.0 + HALF)
            )
            used = jnp.max(jnp.where(reached, meta[6:7], 0.0)) > 0.5

            @pl.when(used)
            def _():
                along_y, along_x = tables(meta, shift_y, shift_x, height, cols, first)
                work(dq, first, cols, t, at, along_y, along_x)

            if skip is not None:

                @pl.when(jnp.logical_not(used))
                def _():
                    skip(t, at)


def forward_kernel(meta_ref, control_ref, mask_ref, out_ref, own, side, ys, xs):
    levels, height, width = control_ref.shape
    half = side.shape[2] // 3
    mask = mask_ref[...].astype(jnp.float32)

    @pl.loop(0, levels)
    def _(l):
        field = control_ref[l] * mask
        hi, lo = split(field)
        at = pl.ds(pl.multiple_of(l * height, height), height)
        own[at, 0:width] = hi
        own[at, width : 2 * width] = hi
        own[at, 2 * width : 3 * width] = lo
        hi = hi.astype(jnp.float32)
        lo = field - hi
        for k, first in enumerate((0, width - half)):
            h, low = hi[:, first : first + half], lo[:, first : first + half]
            side[k, at, :] = jnp.concatenate([h, h, low], axis=1).astype(jnp.bfloat16)

    rows = GROUP * height

    def work(dq, first, cols, t, where, along_y, along_x):
        for i in range(2):
            lanes = slice(i * CHUNK, (i + 1) * CHUNK)
            ys[:, lanes] = along_y[i]
            hi, lo = split(along_x[i])
            xs[0:cols, lanes] = hi
            xs[cols : 2 * cols, lanes] = lo
            xs[2 * cols : 3 * cols, lanes] = hi

        @pl.loop(0, levels // GROUP)
        def _(g):
            at = pl.ds(pl.multiple_of(g * rows, rows), rows)
            left = own[at, :] if dq == 0 else side[(dq + 1) // 2, at, :]
            wide = jnp.dot(left, xs[0 : 3 * cols], preferred_element_type=jnp.float32)
            total = jnp.sum(wide.reshape(GROUP, height, -1) * ys[...][None], axis=1)
            total = total[:, :CHUNK] + total[:, CHUNK:]
            out_ref[t, pl.ds(pl.multiple_of(g * GROUP, GROUP), GROUP), where] = total

    def skip(t, where):
        out_ref[t, :, where] = jnp.zeros((levels, CHUNK), jnp.float32)

    walk(meta_ref, height, width, work, skip)


def backward_kernel(meta_ref, v_ref, control_ref, mask_ref, out_ref, ys, xs):
    levels, height, width = control_ref.shape
    out_ref[...] = jnp.zeros_like(out_ref)
    contract = (((1,), (1,)), ((), ()))

    def work(dq, first, cols, t, where, along_y, along_x):
        if cols < width:
            blank = jnp.zeros((width - cols, CHUNK), jnp.float32)
            order = (lambda x: [x, blank]) if first == 0 else (lambda x: [blank, x])
            along_x = [jnp.concatenate(order(x), axis=0) for x in along_x]
        for i in range(2):
            lanes = slice(i * CHUNK, (i + 1) * CHUNK)
            ys[i] = along_y[i]
            hi, lo = split(along_x[i])
            xs[0:width, lanes] = hi
            xs[width : 2 * width, lanes] = lo

        @pl.loop(0, levels // GROUP)
        def _(g):
            at = pl.ds(pl.multiple_of(g * GROUP, GROUP), GROUP)
            v = v_ref[t, at, where]
            his, los = [], []
            for i in range(2):
                b = (v[:, None, :] * ys[i][None]).reshape(GROUP * height, CHUNK)
                hi, lo = split(b)
                his.append(hi)
                los.append(lo)
            wide = lax.dot_general(
                jnp.concatenate(his, axis=1), xs[...], contract, preferred_element_type=jnp.float32
            )
            rest = lax.dot_general(
                jnp.concatenate(los, axis=1), xs[0:width, :], contract, preferred_element_type=jnp.float32
            )
            total = wide[:, :width] + wide[:, width:] + rest
            out_ref[at] += total.reshape(GROUP, height, width)

    walk(meta_ref, height, width, work)
    mask = mask_ref[...].astype(jnp.float32)

    @pl.loop(0, levels)
    def _(l):
        out_ref[l] = control_ref[l] + mask * out_ref[l]


def to_owner(values):
    return lax.all_to_all(
        lax.all_to_all(values, "lon", split_axis=2, concat_axis=2, tiled=True),
        "lat",
        split_axis=1,
        concat_axis=1,
        tiled=True,
    )


def shards(
    n_lon, n_lat, control, land_mask, std_dev, innovation, inverse_var,
    obs_row, obs_col, frac_row, frac_col, counts,
):
    levels = control.shape[0] * control.shape[1]
    height, width = control.shape[2:]
    slots = obs_row.shape[0] * obs_row.shape[1]
    fields = control.reshape(levels, height, width)
    scales = std_dev.reshape(levels, 1)
    f32 = jnp.float32
    params = functools.partial(pltpu.CompilerParams, vmem_limit_bytes=VMEM_LIMIT)
    sems = pltpu.SemaphoreType.DMA((9,))

    meta, rank = pl.pallas_call(
        meta_kernel,
        out_shape=[jax.ShapeDtypeStruct((8, slots), f32), jax.ShapeDtypeStruct((1, slots), f32)],
        in_specs=[VMEM] * 6,
        out_specs=[VMEM] * 2,
        scratch_shapes=[pltpu.VMEM((8, slots), f32)],
        compiler_params=params(),
        name="slot_weights",
    )(land_mask, obs_row, obs_col, frac_row, frac_col, counts)
    meta_all = pl.pallas_call(
        functools.partial(share_kernel, n_lon, n_lat),
        out_shape=jax.ShapeDtypeStruct((9, 8, slots), f32),
        in_specs=[VMEM],
        out_specs=VMEM,
        scratch_shapes=[sems, sems],
        compiler_params=params(collective_id=0, has_side_effects=True),
        name="share_slots",
    )(meta)

    owned = to_owner(jnp.concatenate([innovation, inverse_var], axis=0)).reshape(2 * levels, slots)

    half = width // 2 if HALF <= width // 2 else width
    parts = pl.pallas_call(
        forward_kernel,
        out_shape=jax.ShapeDtypeStruct((9, levels, slots), f32),
        in_specs=[VMEM] * 3,
        out_specs=VMEM,
        scratch_shapes=[
            pltpu.VMEM((levels * height, 3 * width), jnp.bfloat16),
            pltpu.VMEM((2, levels * height, 3 * half), jnp.bfloat16),
            pltpu.VMEM((height, 2 * CHUNK), f32),
            pltpu.VMEM((3 * width, 2 * CHUNK), jnp.bfloat16),
        ],
        compiler_params=params(),
        name="partial_columns",
    )(meta_all, fields, land_mask)

    scaled = pl.pallas_call(
        functools.partial(misfit_kernel, n_lon, n_lat),
        out_shape=jax.ShapeDtypeStruct((9, levels, slots), f32),
        in_specs=[VMEM] * 5,
        out_specs=VMEM,
        scratch_shapes=[
            pltpu.VMEM((9, levels, slots), f32),
            pltpu.VMEM((levels, slots), f32),
            pltpu.VMEM((2 * levels, slots), f32),
            sems, sems, sems, sems,
        ],
        compiler_params=params(collective_id=1, has_side_effects=True),
        name="misfits",
    )(parts, owned, meta, rank, scales)

    gradient = pl.pallas_call(
        backward_kernel,
        out_shape=jax.ShapeDtypeStruct((levels, height, width), f32),
        in_specs=[VMEM] * 4,
        out_specs=VMEM,
        scratch_shapes=[
            pltpu.VMEM((2, height, CHUNK), f32),
            pltpu.VMEM((2 * width, 2 * CHUNK), jnp.bfloat16),
        ],
        compiler_params=params(),
        name="gradient",
    )(meta_all, scaled, fields, land_mask)
    return gradient.reshape(control.shape)


def solution(mesh):
    tile = P("lat", "lon")
    in_specs = (
        P(None, None, "lat", "lon"), tile, P(),
        P(None, "lat", "lon"), P(None, "lat", "lon"),
        tile, tile, tile, tile, tile,
    )
    body = functools.partial(shards, mesh.shape["lon"], mesh.shape["lat"])
    return jax.shard_map(
        body, mesh=mesh, in_specs=in_specs,
        out_specs=P(None, None, "lat", "lon"), check_vma=False,
    )
```

```python
import functools

import jax
import jax.numpy as jnp
import numpy as np
from jax import lax
from jax.experimental import pallas as pl
from jax.experimental.pallas import tpu as pltpu
from jax.sharding import PartitionSpec as P

HALF = 50
SPREAD = HALF / 2.0
_TAPS = np.exp(-0.5 * (np.arange(-HALF, HALF + 1) / SPREAD) ** 2)
NORM = float(1.0 / np.sqrt(np.sum(_TAPS * _TAPS)))
CHUNK = 128
GROUP = 32
VMEM_LIMIT = 48 * 1024 * 1024
VMEM = pl.BlockSpec(memory_space=pltpu.VMEM)
SMEM = pl.BlockSpec(memory_space=pltpu.SMEM)


def split(x):
    hi = x.astype(jnp.bfloat16)
    lo = (x - hi.astype(jnp.float32)).astype(jnp.bfloat16)
    return hi, lo


def taps(distance):
    values = jnp.exp(distance * distance * (-0.5 / (SPREAD * SPREAD))) * NORM
    return jnp.where(jnp.abs(distance) < HALF + 0.5, values, 0.0)


def iota(shape, dim):
    return lax.broadcasted_iota(jnp.int32, shape, dim).astype(jnp.float32)


def arrange(values, rank, out_ref):
    hi = values.astype(jnp.bfloat16)
    low, least = split(values - hi.astype(jnp.float32))
    parts = jnp.concatenate([hi.astype(jnp.float32), low.astype(jnp.float32), least.astype(jnp.float32)], axis=0)
    parts = parts.astype(jnp.bfloat16)
    count, slots = values.shape
    for k in range(slots // CHUNK):
        place = iota((CHUNK, slots), 0) + float(k * CHUNK)
        one = jnp.where(place == rank, 1.0, 0.0).astype(jnp.bfloat16)
        moved = lax.dot_general(
            parts, one, (((1,), (1,)), ((), ())), preferred_element_type=jnp.float32
        )
        out_ref[:, k * CHUNK : (k + 1) * CHUNK] = (
            moved[:count] + moved[count : 2 * count] + moved[2 * count :]
        )


def meta_kernel(mask_ref, row_ref, col_ref, frow_ref, fcol_ref, counts_ref, out_ref, rank_ref, raw):
    mask = mask_ref[...].astype(jnp.bfloat16)
    height, width = mask.shape
    holders, lanes = row_ref.shape
    tiles = counts_ref.shape[1]
    cap = lanes // tiles
    tile = lax.broadcasted_iota(jnp.int32, (tiles, lanes), 0)
    lane = lax.broadcasted_iota(jnp.int32, (tiles, lanes), 1)
    inside = (lane >= tile * cap) & (lane < tile * cap + cap)
    repeat = jnp.where(inside, 1.0, 0.0).astype(jnp.bfloat16)
    first = jnp.sum(jnp.where(inside, tile * cap, 0).astype(jnp.float32), axis=0, keepdims=True)
    number = iota((1, lanes), 1) - first
    limits = jnp.dot(
        counts_ref[...].astype(jnp.float32).astype(jnp.bfloat16),
        repeat,
        preferred_element_type=jnp.float32,
    )
    for s in range(holders):
        row = row_ref[pl.ds(s, 1), :].astype(jnp.float32)
        col = col_ref[pl.ds(s, 1), :].astype(jnp.float32)
        a = frow_ref[pl.ds(s, 1), :]
        b = fcol_ref[pl.ds(s, 1), :]
        x = iota((width, lanes), 0) - col
        at_left = jnp.where(x == 0.0, 1.0, 0.0).astype(jnp.bfloat16)
        at_right = jnp.where(x == 1.0, 1.0, 0.0).astype(jnp.bfloat16)
        left = jnp.dot(mask, at_left, preferred_element_type=jnp.float32)
        right = jnp.dot(mask, at_right, preferred_element_type=jnp.float32)
        y = iota((height, lanes), 0) - row
        m00 = jnp.sum(jnp.where(y == 0.0, left, 0.0), axis=0, keepdims=True)
        m01 = jnp.sum(jnp.where(y == 0.0, right, 0.0), axis=0, keepdims=True)
        m10 = jnp.sum(jnp.where(y == 1.0, left, 0.0), axis=0, keepdims=True)
        m11 = jnp.sum(jnp.where(y == 1.0, right, 0.0), axis=0, keepdims=True)
        live = jnp.where(number < limits[s : s + 1], 1.0, 0.0)
        at = pl.ds(s * lanes, lanes)
        raw[0:1, at] = row
        raw[1:2, at] = col
        raw[2:3, at] = (1.0 - a) * (1.0 - b) * m00 * live
        raw[3:4, at] = (1.0 - a) * b * m01 * live
        raw[4:5, at] = a * (1.0 - b) * m10 * live
        raw[5:6, at] = a * b * m11 * live
        raw[6:7, at] = live
        raw[7:8, at] = live


    slots = raw.shape[1]
    order = jnp.where(raw[6:7, :] > 0.0, raw[1:2, :], float(width)) * slots + iota((1, slots), 1)
    eye = iota((CHUNK, CHUNK), 0) == iota((CHUNK, CHUNK), 1)
    rank = jnp.zeros((1, slots), jnp.float32)
    for k in range(slots // CHUNK):
        piece = order[:, k * CHUNK : (k + 1) * CHUNK]
        column = jnp.sum(jnp.where(eye, piece, 0.0), axis=1, keepdims=True)
        rank = rank + jnp.sum(jnp.where(column < order, 1.0, 0.0), axis=0, keepdims=True)
    rank_ref[...] = rank
    arrange(raw[...], rank, out_ref)


def neighbours(n_lon, n_lat):
    lon, lat = lax.axis_index("lon"), lax.axis_index("lat")
    found = []
    for t in range(9):
        if t == 4:
            continue
        dp, dq = t // 3 - 1, t % 3 - 1
        there = (lat + dp >= 0) & (lat + dp < n_lat)
        target = {"lon": lax.rem(lon + dq + n_lon, n_lon), "lat": lat + dp}
        found.append((t, there, target, dp))
    return found


def guarded(dp, there, body):
    if dp == 0:
        body()
    else:
        pl.when(there)(body)


def greet(near):
    barrier = pltpu.get_barrier_semaphore()
    for _, there, target, dp in near:
        guarded(dp, there, lambda target=target: pl.semaphore_signal(barrier, inc=1, device_id=target))
    peers = sum(jnp.where(there, 1, 0) for _, there, _, _ in near)
    pl.semaphore_wait(barrier, peers)


def exchange(near, source, target_ref, send_sem, recv_sem):
    copies = []
    for t, there, target, dp in near:
        copy = pltpu.make_async_remote_copy(
            src_ref=source(t),
            dst_ref=target_ref.at[8 - t],
            send_sem=send_sem.at[t],
            recv_sem=recv_sem.at[8 - t],
            device_id=target,
        )
        guarded(dp, there, copy.start)
        copies.append((t, there, dp, copy))
    return copies


def finish(near, copies, target_ref, recv_sem):
    for t, there, dp, copy in copies:
        guarded(dp, there, copy.wait_send)
    for t, there, target, dp in near:
        arrival = pltpu.make_async_remote_copy(
            src_ref=target_ref.at[t],
            dst_ref=target_ref.at[t],
            send_sem=recv_sem.at[t],
            recv_sem=recv_sem.at[t],
            device_id=target,
        )
        guarded(dp, there, arrival.wait_recv)


def clear_missing(near, ref):
    for t, there, _, dp in near:
        if dp == 0:
            continue

        @pl.when(jnp.logical_not(there))
        def _():
            ref[t] = jnp.zeros(ref.shape[1:], ref.dtype)


def share_kernel(n_lon, n_lat, height, width, meta_ref, out_ref, used_ref, send_sem, recv_sem):
    near = neighbours(n_lon, n_lat)
    greet(near)
    copies = exchange(near, lambda t: meta_ref, out_ref, send_sem, recv_sem)
    out_ref[4] = meta_ref[...]
    clear_missing(near, out_ref)
    finish(near, copies, out_ref, recv_sem)
    slots = out_ref.shape[2]
    for t in range(9):
        meta = out_ref[t]
        y, x = meta[0:1] + float((t // 3 - 1) * height), meta[1:2] + float((t % 3 - 1) * width)
        reached = (
            (y >= -(HALF + 1.0)) & (y <= height - 1.0 + HALF)
            & (x >= -(HALF + 1.0)) & (x <= width - 1.0 + HALF)
        )
        live = jnp.where(reached, meta[6:7], 0.0)
        for c in range(slots // CHUNK):
            used_ref[t : t + 1, c : c + 1] = jnp.max(
                live[:, c * CHUNK : (c + 1) * CHUNK], axis=1, keepdims=True
            )


def misfit_kernel(
    n_lon, n_lat, part_ref, owned_ref, meta_ref, rank_ref, std_ref, out_ref,
    landed, mine, placed, send_sem, recv_sem, send_sem_2, recv_sem_2,
):
    near = neighbours(n_lon, n_lat)
    greet(near)
    copies = exchange(near, lambda t: part_ref.at[t], landed, send_sem, recv_sem)
    clear_missing(near, landed)
    clear_missing(near, out_ref)
    arrange(owned_ref[...], rank_ref[...], placed)
    finish(near, copies, landed, recv_sem)
    total = part_ref[4]
    for t in range(9):
        if t != 4:
            total = total + landed[t]
    rows = total.shape[0]
    scale = std_ref[...]
    live = meta_ref[6:7, :]
    mine[...] = scale * placed[rows:, :] * (scale * total - placed[:rows, :]) * live
    out_ref[4] = mine[...]
    copies = exchange(near, lambda t: mine, out_ref, send_sem_2, recv_sem_2)
    finish(near, copies, out_ref, recv_sem_2)


def tables(meta, shift_y, shift_x, height, width, first):
    chunk = meta.shape[1]
    y = meta[0:1] + shift_y - iota((height, chunk), 0)
    x = meta[1:2] + shift_x - first - iota((width, chunk), 0)
    left, right = taps(x), taps(x + 1.0)
    along_x = [
        meta[2:3] * left + meta[3:4] * right,
        meta[4:5] * left + meta[5:6] * right,
    ]
    return [taps(y), taps(y + 1.0)], along_x


def walk(meta_ref, used_ref, height, width, work, skip=None):
    chunks = meta_ref.shape[2] // CHUNK
    near_cols = width // 2 if HALF <= width // 2 else width
    for dq in (-1, 0, 1):
        cols = near_cols if dq else width
        first = width - cols if dq > 0 else 0

        @pl.loop(0, 3 * chunks)
        def _(step):
            p, c = lax.div(step, chunks), lax.rem(step, chunks)
            t = 3 * p + (dq + 1)
            at = pl.ds(pl.multiple_of(c * CHUNK, CHUNK), CHUNK)
            meta = meta_ref[t, :, at]
            shift_y = (p - 1).astype(jnp.float32) * height
            shift_x = float(dq * width)
            used = used_ref[t, c] > 0.5

            @pl.when(used)
            def _():
                along_y, along_x = tables(meta, shift_y, shift_x, height, cols, first)
                work(dq, first, cols, t, at, along_y, along_x)

            if skip is not None:

                @pl.when(jnp.logical_not(used))
                def _():
                    skip(t, at)


def forward_kernel(meta_ref, used_ref, control_ref, mask_ref, out_ref, own, side, ys, xs):
    levels, height, width = control_ref.shape
    half = side.shape[2] // 3
    mask = mask_ref[...].astype(jnp.float32)

    @pl.loop(0, levels)
    def _(l):
        field = control_ref[l] * mask
        hi, lo = split(field)
        at = pl.ds(pl.multiple_of(l * height, height), height)
        own[at, 0:width] = hi
        own[at, width : 2 * width] = hi
        own[at, 2 * width : 3 * width] = lo
        hi = hi.astype(jnp.float32)
        lo = field - hi
        for k, first in enumerate((0, width - half)):
            h, low = hi[:, first : first + half], lo[:, first : first + half]
            side[k, at, :] = jnp.concatenate([h, h, low], axis=1).astype(jnp.bfloat16)

    rows = GROUP * height

    def work(dq, first, cols, t, where, along_y, along_x):
        for i in range(2):
            lanes = slice(i * CHUNK, (i + 1) * CHUNK)
            ys[:, lanes] = along_y[i]
            hi, lo = split(along_x[i])
            xs[0:cols, lanes] = hi
            xs[cols : 2 * cols, lanes] = lo
            xs[2 * cols : 3 * cols, lanes] = hi

        @pl.loop(0, levels // GROUP)
        def _(g):
            at = pl.ds(pl.multiple_of(g * rows, rows), rows)
            left = own[at, :] if dq == 0 else side[(dq + 1) // 2, at, :]
            wide = jnp.dot(left, xs[0 : 3 * cols], preferred_element_type=jnp.float32)
            total = jnp.sum(wide.reshape(GROUP, height, -1) * ys[...][None], axis=1)
            total = total[:, :CHUNK] + total[:, CHUNK:]
            out_ref[t, pl.ds(pl.multiple_of(g * GROUP, GROUP), GROUP), where] = total

    def skip(t, where):
        out_ref[t, :, where] = jnp.zeros((levels, CHUNK), jnp.float32)

    walk(meta_ref, used_ref, height, width, work, skip)


def backward_kernel(meta_ref, used_ref, v_ref, control_ref, mask_ref, out_ref, ys, xs):
    levels, height, width = control_ref.shape
    out_ref[...] = jnp.zeros_like(out_ref)
    contract = (((1,), (1,)), ((), ()))

    def work(dq, first, cols, t, where, along_y, along_x):
        if cols < width:
            blank = jnp.zeros((width - cols, CHUNK), jnp.float32)
            order = (lambda x: [x, blank]) if first == 0 else (lambda x: [blank, x])
            along_x = [jnp.concatenate(order(x), axis=0) for x in along_x]
        for i in range(2):
            lanes = slice(i * CHUNK, (i + 1) * CHUNK)
            ys[i] = along_y[i]
            hi, lo = split(along_x[i])
            xs[0:width, lanes] = hi
            xs[width : 2 * width, lanes] = lo

        @pl.loop(0, levels // GROUP)
        def _(g):
            at = pl.ds(pl.multiple_of(g * GROUP, GROUP), GROUP)
            v = v_ref[t, at, where]
            his, los = [], []
            for i in range(2):
                b = (v[:, None, :] * ys[i][None]).reshape(GROUP * height, CHUNK)
                hi, lo = split(b)
                his.append(hi)
                los.append(lo)
            wide = lax.dot_general(
                jnp.concatenate(his, axis=1), xs[...], contract, preferred_element_type=jnp.float32
            )
            rest = lax.dot_general(
                jnp.concatenate(los, axis=1), xs[0:width, :], contract, preferred_element_type=jnp.float32
            )
            total = wide[:, :width] + wide[:, width:] + rest
            out_ref[at] += total.reshape(GROUP, height, width)

    walk(meta_ref, used_ref, height, width, work)
    mask = mask_ref[...].astype(jnp.float32)

    @pl.loop(0, levels)
    def _(l):
        out_ref[l] = control_ref[l] + mask * out_ref[l]


def to_owner(values, n_lat, n_lon):
    count, cap = values.shape[0], values.shape[2] // n_lon
    blocks = values.reshape(count, n_lat, n_lon, cap).transpose(1, 2, 0, 3)
    blocks = blocks.reshape(n_lat * n_lon, count * cap)
    moved = lax.all_to_all(blocks, ("lat", "lon"), split_axis=0, concat_axis=0, tiled=True)
    return moved.reshape(n_lat * n_lon, count, cap).transpose(1, 0, 2).reshape(count, -1)


def shards(
    n_lon, n_lat, control, land_mask, std_dev, innovation, inverse_var,
    obs_row, obs_col, frac_row, frac_col, counts,
):
    levels = control.shape[0] * control.shape[1]
    height, width = control.shape[2:]
    slots = obs_row.shape[0] * obs_row.shape[1]
    fields = control.reshape(levels, height, width)
    scales = std_dev.reshape(levels, 1)
    f32 = jnp.float32
    params = functools.partial(pltpu.CompilerParams, vmem_limit_bytes=VMEM_LIMIT)
    sems = pltpu.SemaphoreType.DMA((9,))

    meta, rank = pl.pallas_call(
        meta_kernel,
        out_shape=[jax.ShapeDtypeStruct((8, slots), f32), jax.ShapeDtypeStruct((1, slots), f32)],
        in_specs=[VMEM] * 6,
        out_specs=[VMEM] * 2,
        scratch_shapes=[pltpu.VMEM((8, slots), f32)],
        compiler_params=params(),
        name="slot_weights",
    )(land_mask, obs_row, obs_col, frac_row, frac_col, counts)
    meta_all, used = pl.pallas_call(
        functools.partial(share_kernel, n_lon, n_lat, height, width),
        out_shape=[
            jax.ShapeDtypeStruct((9, 8, slots), f32),
            jax.ShapeDtypeStruct((9, slots // CHUNK), f32),
        ],
        in_specs=[VMEM],
        out_specs=[VMEM] * 2,
        scratch_shapes=[sems, sems],
        compiler_params=params(collective_id=0, has_side_effects=True),
        name="share_slots",
    )(meta)

    owned = to_owner(jnp.concatenate([innovation, inverse_var], axis=0), n_lat, n_lon)

    half = width // 2 if HALF <= width // 2 else width
    parts = pl.pallas_call(
        forward_kernel,
        out_shape=jax.ShapeDtypeStruct((9, levels, slots), f32),
        in_specs=[VMEM, SMEM, VMEM, VMEM],
        out_specs=VMEM,
        scratch_shapes=[
            pltpu.VMEM((levels * height, 3 * width), jnp.bfloat16),
            pltpu.VMEM((2, levels * height, 3 * half), jnp.bfloat16),
            pltpu.VMEM((height, 2 * CHUNK), f32),
            pltpu.VMEM((3 * width, 2 * CHUNK), jnp.bfloat16),
        ],
        compiler_params=params(),
        name="partial_columns",
    )(meta_all, used, fields, land_mask)

    scaled = pl.pallas_call(
        functools.partial(misfit_kernel, n_lon, n_lat),
        out_shape=jax.ShapeDtypeStruct((9, levels, slots), f32),
        in_specs=[VMEM] * 5,
        out_specs=VMEM,
        scratch_shapes=[
            pltpu.VMEM((9, levels, slots), f32),
            pltpu.VMEM((levels, slots), f32),
            pltpu.VMEM((2 * levels, slots), f32),
            sems, sems, sems, sems,
        ],
        compiler_params=params(collective_id=1, has_side_effects=True),
        name="misfits",
    )(parts, owned, meta, rank, scales)

    gradient = pl.pallas_call(
        backward_kernel,
        out_shape=jax.ShapeDtypeStruct((levels, height, width), f32),
        in_specs=[VMEM, SMEM, VMEM, VMEM, VMEM],
        out_specs=VMEM,
        scratch_shapes=[
            pltpu.VMEM((2, height, CHUNK), f32),
            pltpu.VMEM((2 * width, 2 * CHUNK), jnp.bfloat16),
        ],
        compiler_params=params(),
        name="gradient",
    )(meta_all, used, scaled, fields, land_mask)
    return gradient.reshape(control.shape)


def solution(mesh):
    tile = P("lat", "lon")
    in_specs = (
        P(None, None, "lat", "lon"), tile, P(),
        P(None, "lat", "lon"), P(None, "lat", "lon"),
        tile, tile, tile, tile, tile,
    )
    body = functools.partial(shards, mesh.shape["lon"], mesh.shape["lat"])
    return jax.shard_map(
        body, mesh=mesh, in_specs=in_specs,
        out_specs=P(None, None, "lat", "lon"), check_vma=False,
    )
```

```python
import functools

import jax
import jax.numpy as jnp
import numpy as np
from jax import lax
from jax.experimental import pallas as pl
from jax.experimental.pallas import tpu as pltpu
from jax.sharding import PartitionSpec as P

HALF = 50
SPREAD = HALF / 2.0
_TAPS = np.exp(-0.5 * (np.arange(-HALF, HALF + 1) / SPREAD) ** 2)
NORM = float(1.0 / np.sqrt(np.sum(_TAPS * _TAPS)))
CHUNK = 128
GROUP = 32
VMEM_LIMIT = 48 * 1024 * 1024
VMEM = pl.BlockSpec(memory_space=pltpu.VMEM)
SMEM = pl.BlockSpec(memory_space=pltpu.SMEM)


def split(x):
    hi = x.astype(jnp.bfloat16)
    lo = (x - hi.astype(jnp.float32)).astype(jnp.bfloat16)
    return hi, lo


def taps(distance):
    values = jnp.exp(distance * distance * (-0.5 / (SPREAD * SPREAD))) * NORM
    return jnp.where(jnp.abs(distance) < HALF + 0.5, values, 0.0)


def iota(shape, dim):
    return lax.broadcasted_iota(jnp.int32, shape, dim).astype(jnp.float32)


def arrange(values, rank, out_ref):
    hi = values.astype(jnp.bfloat16)
    low, least = split(values - hi.astype(jnp.float32))
    parts = jnp.concatenate([hi.astype(jnp.float32), low.astype(jnp.float32), least.astype(jnp.float32)], axis=0)
    parts = parts.astype(jnp.bfloat16)
    count, slots = values.shape
    for k in range(slots // CHUNK):
        place = iota((CHUNK, slots), 0) + float(k * CHUNK)
        one = jnp.where(place == rank, 1.0, 0.0).astype(jnp.bfloat16)
        moved = lax.dot_general(
            parts, one, (((1,), (1,)), ((), ())), preferred_element_type=jnp.float32
        )
        out_ref[:, k * CHUNK : (k + 1) * CHUNK] = (
            moved[:count] + moved[count : 2 * count] + moved[2 * count :]
        )


def meta_kernel(mask_ref, row_ref, col_ref, frow_ref, fcol_ref, counts_ref, out_ref, rank_ref, raw):
    mask = mask_ref[...].astype(jnp.bfloat16)
    height, width = mask.shape
    holders, lanes = row_ref.shape
    tiles = counts_ref.shape[1]
    cap = lanes // tiles
    tile = lax.broadcasted_iota(jnp.int32, (tiles, lanes), 0)
    lane = lax.broadcasted_iota(jnp.int32, (tiles, lanes), 1)
    inside = (lane >= tile * cap) & (lane < tile * cap + cap)
    repeat = jnp.where(inside, 1.0, 0.0).astype(jnp.bfloat16)
    first = jnp.sum(jnp.where(inside, tile * cap, 0).astype(jnp.float32), axis=0, keepdims=True)
    number = iota((1, lanes), 1) - first
    limits = jnp.dot(
        counts_ref[...].astype(jnp.float32).astype(jnp.bfloat16),
        repeat,
        preferred_element_type=jnp.float32,
    )
    for s in range(holders):
        row = row_ref[pl.ds(s, 1), :].astype(jnp.float32)
        col = col_ref[pl.ds(s, 1), :].astype(jnp.float32)
        a = frow_ref[pl.ds(s, 1), :]
        b = fcol_ref[pl.ds(s, 1), :]
        x = iota((width, lanes), 0) - col
        at_left = jnp.where(x == 0.0, 1.0, 0.0).astype(jnp.bfloat16)
        at_right = jnp.where(x == 1.0, 1.0, 0.0).astype(jnp.bfloat16)
        left = jnp.dot(mask, at_left, preferred_element_type=jnp.float32)
        right = jnp.dot(mask, at_right, preferred_element_type=jnp.float32)
        y = iota((height, lanes), 0) - row
        m00 = jnp.sum(jnp.where(y == 0.0, left, 0.0), axis=0, keepdims=True)
        m01 = jnp.sum(jnp.where(y == 0.0, right, 0.0), axis=0, keepdims=True)
        m10 = jnp.sum(jnp.where(y == 1.0, left, 0.0), axis=0, keepdims=True)
        m11 = jnp.sum(jnp.where(y == 1.0, right, 0.0), axis=0, keepdims=True)
        live = jnp.where(number < limits[s : s + 1], 1.0, 0.0)
        at = pl.ds(s * lanes, lanes)
        raw[0:1, at] = row
        raw[1:2, at] = col
        raw[2:3, at] = (1.0 - a) * (1.0 - b) * m00 * live
        raw[3:4, at] = (1.0 - a) * b * m01 * live
        raw[4:5, at] = a * (1.0 - b) * m10 * live
        raw[5:6, at] = a * b * m11 * live
        raw[6:7, at] = live
        raw[7:8, at] = live


    slots = raw.shape[1]
    order = jnp.where(raw[6:7, :] > 0.0, raw[1:2, :], float(width)) * slots + iota((1, slots), 1)
    eye = iota((CHUNK, CHUNK), 0) == iota((CHUNK, CHUNK), 1)
    rank = jnp.zeros((1, slots), jnp.float32)
    for k in range(slots // CHUNK):
        piece = order[:, k * CHUNK : (k + 1) * CHUNK]
        column = jnp.sum(jnp.where(eye, piece, 0.0), axis=1, keepdims=True)
        rank = rank + jnp.sum(jnp.where(column < order, 1.0, 0.0), axis=0, keepdims=True)
    rank_ref[...] = rank
    arrange(raw[...], rank, out_ref)


def neighbours(n_lon, n_lat):
    lon, lat = lax.axis_index("lon"), lax.axis_index("lat")
    found = []
    for t in range(9):
        if t == 4:
            continue
        dp, dq = t // 3 - 1, t % 3 - 1
        there = (lat + dp >= 0) & (lat + dp < n_lat)
        target = {"lon": lax.rem(lon + dq + n_lon, n_lon), "lat": lat + dp}
        found.append((t, there, target, dp))
    return found


def guarded(dp, there, body):
    if dp == 0:
        body()
    else:
        pl.when(there)(body)


def greet(near, between=None):
    barrier = pltpu.get_barrier_semaphore()
    for _, there, target, dp in near:
        guarded(dp, there, lambda target=target: pl.semaphore_signal(barrier, inc=1, device_id=target))
    if between is not None:
        between()
    peers = sum(jnp.where(there, 1, 0) for _, there, _, _ in near)
    pl.semaphore_wait(barrier, peers)


def exchange(near, source, target_ref, send_sem, recv_sem):
    copies = []
    for t, there, target, dp in near:
        copy = pltpu.make_async_remote_copy(
            src_ref=source(t),
            dst_ref=target_ref.at[8 - t],
            send_sem=send_sem.at[t],
            recv_sem=recv_sem.at[8 - t],
            device_id=target,
        )
        guarded(dp, there, copy.start)
        copies.append((t, there, dp, copy))
    return copies


def finish(near, copies, target_ref, recv_sem):
    for t, there, dp, copy in copies:
        guarded(dp, there, copy.wait_send)
    for t, there, target, dp in near:
        arrival = pltpu.make_async_remote_copy(
            src_ref=target_ref.at[t],
            dst_ref=target_ref.at[t],
            send_sem=recv_sem.at[t],
            recv_sem=recv_sem.at[t],
            device_id=target,
        )
        guarded(dp, there, arrival.wait_recv)


def clear_missing(near, ref):
    for t, there, _, dp in near:
        if dp == 0:
            continue

        @pl.when(jnp.logical_not(there))
        def _():
            ref[t] = jnp.zeros(ref.shape[1:], ref.dtype)


def share_kernel(n_lon, n_lat, *refs):
    inputs, (meta_ref, rank_ref, out_ref, used_ref, raw, send_sem, recv_sem) = refs[:6], refs[6:]
    height, width = inputs[0].shape
    near = neighbours(n_lon, n_lat)
    greet(near, lambda: meta_kernel(*inputs, meta_ref, rank_ref, raw))
    copies = exchange(near, lambda t: meta_ref, out_ref, send_sem, recv_sem)
    out_ref[4] = meta_ref[...]
    clear_missing(near, out_ref)
    finish(near, copies, out_ref, recv_sem)
    slots = out_ref.shape[2]
    for t in range(9):
        meta = out_ref[t]
        y, x = meta[0:1] + float((t // 3 - 1) * height), meta[1:2] + float((t % 3 - 1) * width)
        reached = (
            (y >= -(HALF + 1.0)) & (y <= height - 1.0 + HALF)
            & (x >= -(HALF + 1.0)) & (x <= width - 1.0 + HALF)
        )
        live = jnp.where(reached, meta[6:7], 0.0)
        for c in range(slots // CHUNK):
            used_ref[t : t + 1, c : c + 1] = jnp.max(
                live[:, c * CHUNK : (c + 1) * CHUNK], axis=1, keepdims=True
            )


def misfit_kernel(
    n_lon, n_lat, part_ref, owned_ref, meta_ref, rank_ref, std_ref, out_ref,
    landed, mine, placed, send_sem, recv_sem, send_sem_2, recv_sem_2,
):
    near = neighbours(n_lon, n_lat)
    greet(near)
    copies = exchange(near, lambda t: part_ref.at[t], landed, send_sem, recv_sem)
    clear_missing(near, landed)
    clear_missing(near, out_ref)
    arrange(owned_ref[...], rank_ref[...], placed)
    finish(near, copies, landed, recv_sem)
    total = part_ref[4]
    for t in range(9):
        if t != 4:
            total = total + landed[t]
    rows = total.shape[0]
    scale = std_ref[...]
    live = meta_ref[6:7, :]
    mine[...] = scale * placed[rows:, :] * (scale * total - placed[:rows, :]) * live
    out_ref[4] = mine[...]
    copies = exchange(near, lambda t: mine, out_ref, send_sem_2, recv_sem_2)
    finish(near, copies, out_ref, recv_sem_2)


def tables(meta, shift_y, shift_x, height, width, first):
    chunk = meta.shape[1]
    y = meta[0:1] + shift_y - iota((height, chunk), 0)
    x = meta[1:2] + shift_x - first - iota((width, chunk), 0)
    left, right = taps(x), taps(x + 1.0)
    along_x = [
        meta[2:3] * left + meta[3:4] * right,
        meta[4:5] * left + meta[5:6] * right,
    ]
    return [taps(y), taps(y + 1.0)], along_x


def walk(meta_ref, used_ref, height, width, work, skip=None):
    chunks = meta_ref.shape[2] // CHUNK
    near_cols = width // 2 if HALF <= width // 2 else width
    for dq in (-1, 0, 1):
        cols = near_cols if dq else width
        first = width - cols if dq > 0 else 0

        @pl.loop(0, 3 * chunks)
        def _(step):
            p, c = lax.div(step, chunks), lax.rem(step, chunks)
            t = 3 * p + (dq + 1)
            at = pl.ds(pl.multiple_of(c * CHUNK, CHUNK), CHUNK)
            meta = meta_ref[t, :, at]
            shift_y = (p - 1).astype(jnp.float32) * height
            shift_x = float(dq * width)
            used = used_ref[t, c] > 0.5

            @pl.when(used)
            def _():
                along_y, along_x = tables(meta, shift_y, shift_x, height, cols, first)
                work(dq, first, cols, t, at, along_y, along_x)

            if skip is not None:

                @pl.when(jnp.logical_not(used))
                def _():
                    skip(t, at)


def forward_kernel(meta_ref, used_ref, control_ref, mask_ref, out_ref, own, side, ys, xs):
    levels, height, width = control_ref.shape
    half = side.shape[2] // 3
    mask = mask_ref[...].astype(jnp.float32)

    @pl.loop(0, levels, unroll=8)
    def _(l):
        field = control_ref[l] * mask
        hi, lo = split(field)
        at = pl.ds(pl.multiple_of(l * height, height), height)
        own[at, 0:width] = hi
        own[at, width : 2 * width] = hi
        own[at, 2 * width : 3 * width] = lo
        hi = hi.astype(jnp.float32)
        lo = field - hi
        for k, first in enumerate((0, width - half)):
            h, low = hi[:, first : first + half], lo[:, first : first + half]
            side[k, at, :] = jnp.concatenate([h, h, low], axis=1).astype(jnp.bfloat16)

    rows = GROUP * height

    def work(dq, first, cols, t, where, along_y, along_x):
        for i in range(2):
            lanes = slice(i * CHUNK, (i + 1) * CHUNK)
            ys[:, lanes] = along_y[i]
            hi, lo = split(along_x[i])
            xs[0:cols, lanes] = hi
            xs[cols : 2 * cols, lanes] = lo
            xs[2 * cols : 3 * cols, lanes] = hi

        @pl.loop(0, levels // GROUP)
        def _(g):
            at = pl.ds(pl.multiple_of(g * rows, rows), rows)
            left = own[at, :] if dq == 0 else side[(dq + 1) // 2, at, :]
            wide = jnp.dot(left, xs[0 : 3 * cols], preferred_element_type=jnp.float32)
            total = jnp.sum(wide.reshape(GROUP, height, -1) * ys[...][None], axis=1)
            total = total[:, :CHUNK] + total[:, CHUNK:]
            out_ref[t, pl.ds(pl.multiple_of(g * GROUP, GROUP), GROUP), where] = total

    def skip(t, where):
        out_ref[t, :, where] = jnp.zeros((levels, CHUNK), jnp.float32)

    walk(meta_ref, used_ref, height, width, work, skip)


def backward_kernel(meta_ref, used_ref, v_ref, control_ref, mask_ref, out_ref, ys, xs):
    levels, height, width = control_ref.shape
    out_ref[...] = jnp.zeros_like(out_ref)
    contract = (((1,), (1,)), ((), ()))

    def work(dq, first, cols, t, where, along_y, along_x):
        if cols < width:
            blank = jnp.zeros((width - cols, CHUNK), jnp.float32)
            order = (lambda x: [x, blank]) if first == 0 else (lambda x: [blank, x])
            along_x = [jnp.concatenate(order(x), axis=0) for x in along_x]
        for i in range(2):
            lanes = slice(i * CHUNK, (i + 1) * CHUNK)
            ys[i] = along_y[i]
            hi, lo = split(along_x[i])
            xs[0:width, lanes] = hi
            xs[width : 2 * width, lanes] = lo

        @pl.loop(0, levels // GROUP)
        def _(g):
            at = pl.ds(pl.multiple_of(g * GROUP, GROUP), GROUP)
            v = v_ref[t, at, where]
            his, los = [], []
            for i in range(2):
                b = (v[:, None, :] * ys[i][None]).reshape(GROUP * height, CHUNK)
                hi, lo = split(b)
                his.append(hi)
                los.append(lo)
            wide = lax.dot_general(
                jnp.concatenate(his, axis=1), xs[...], contract, preferred_element_type=jnp.float32
            )
            rest = lax.dot_general(
                jnp.concatenate(los, axis=1), xs[0:width, :], contract, preferred_element_type=jnp.float32
            )
            total = wide[:, :width] + wide[:, width:] + rest
            out_ref[at] += total.reshape(GROUP, height, width)

    walk(meta_ref, used_ref, height, width, work)
    mask = mask_ref[...].astype(jnp.float32)

    @pl.loop(0, levels, unroll=8)
    def _(l):
        out_ref[l] = control_ref[l] + mask * out_ref[l]


def to_owner(values, n_lat, n_lon):
    count, cap = values.shape[0], values.shape[2] // n_lon
    blocks = values.reshape(count, n_lat, n_lon, cap).transpose(1, 2, 0, 3)
    blocks = blocks.reshape(n_lat * n_lon, count * cap)
    moved = lax.all_to_all(blocks, ("lat", "lon"), split_axis=0, concat_axis=0, tiled=True)
    return moved.reshape(n_lat * n_lon, count, cap).transpose(1, 0, 2).reshape(count, -1)


def shards(
    n_lon, n_lat, control, land_mask, std_dev, innovation, inverse_var,
    obs_row, obs_col, frac_row, frac_col, counts,
):
    levels = control.shape[0] * control.shape[1]
    height, width = control.shape[2:]
    slots = obs_row.shape[0] * obs_row.shape[1]
    fields = control.reshape(levels, height, width)
    scales = std_dev.reshape(levels, 1)
    f32 = jnp.float32
    params = functools.partial(pltpu.CompilerParams, vmem_limit_bytes=VMEM_LIMIT)
    sems = pltpu.SemaphoreType.DMA((9,))

    meta, rank, meta_all, used = pl.pallas_call(
        functools.partial(share_kernel, n_lon, n_lat),
        out_shape=[
            jax.ShapeDtypeStruct((8, slots), f32),
            jax.ShapeDtypeStruct((1, slots), f32),
            jax.ShapeDtypeStruct((9, 8, slots), f32),
            jax.ShapeDtypeStruct((9, slots // CHUNK), f32),
        ],
        in_specs=[VMEM] * 6,
        out_specs=[VMEM] * 4,
        scratch_shapes=[pltpu.VMEM((8, slots), f32), sems, sems],
        compiler_params=params(collective_id=0, has_side_effects=True),
        name="share_slots",
    )(land_mask, obs_row, obs_col, frac_row, frac_col, counts)

    owned = to_owner(jnp.concatenate([innovation, inverse_var], axis=0), n_lat, n_lon)

    half = width // 2 if HALF <= width // 2 else width
    parts = pl.pallas_call(
        forward_kernel,
        out_shape=jax.ShapeDtypeStruct((9, levels, slots), f32),
        in_specs=[VMEM, SMEM, VMEM, VMEM],
        out_specs=VMEM,
        scratch_shapes=[
            pltpu.VMEM((levels * height, 3 * width), jnp.bfloat16),
            pltpu.VMEM((2, levels * height, 3 * half), jnp.bfloat16),
            pltpu.VMEM((height, 2 * CHUNK), f32),
            pltpu.VMEM((3 * width, 2 * CHUNK), jnp.bfloat16),
        ],
        compiler_params=params(),
        name="partial_columns",
    )(meta_all, used, fields, land_mask)

    scaled = pl.pallas_call(
        functools.partial(misfit_kernel, n_lon, n_lat),
        out_shape=jax.ShapeDtypeStruct((9, levels, slots), f32),
        in_specs=[VMEM] * 5,
        out_specs=VMEM,
        scratch_shapes=[
            pltpu.VMEM((9, levels, slots), f32),
            pltpu.VMEM((levels, slots), f32),
            pltpu.VMEM((2 * levels, slots), f32),
            sems, sems, sems, sems,
        ],
        compiler_params=params(collective_id=1, has_side_effects=True),
        name="misfits",
    )(parts, owned, meta, rank, scales)

    gradient = pl.pallas_call(
        backward_kernel,
        out_shape=jax.ShapeDtypeStruct((levels, height, width), f32),
        in_specs=[VMEM, SMEM, VMEM, VMEM, VMEM],
        out_specs=VMEM,
        scratch_shapes=[
            pltpu.VMEM((2, height, CHUNK), f32),
            pltpu.VMEM((2 * width, 2 * CHUNK), jnp.bfloat16),
        ],
        compiler_params=params(),
        name="gradient",
    )(meta_all, used, scaled, fields, land_mask)
    return gradient.reshape(control.shape)


def solution(mesh):
    tile = P("lat", "lon")
    in_specs = (
        P(None, None, "lat", "lon"), tile, P(),
        P(None, "lat", "lon"), P(None, "lat", "lon"),
        tile, tile, tile, tile, tile,
    )
    body = functools.partial(shards, mesh.shape["lon"], mesh.shape["lat"])
    return jax.shard_map(
        body, mesh=mesh, in_specs=in_specs,
        out_specs=P(None, None, "lat", "lon"), check_vma=False,
    )
```
